32 devices in a mesh: tmpl: 4 (over y, x), tm: 4 (over z), rec: 2 (over core).
Axes of the slice: x: 2, y: 2, z: 4, core: 2. Of those that a mesh axis runs over, the one named last changes fastest.
Arguments:
- corpus: bfloat16 [8, 8192, 128], P(('tmpl', 'rec'), 'tm'), may hold values from -16 to 16
- templates: bfloat16 [512, 64, 128], P(('tmpl', 'rec')), may hold values from -4 to 4
- rec_ids: int32 [8, 8192], P(('tmpl', 'rec'), 'tm'), may hold values from 0 to 15, never falling along the last dimension, each value on 1 to 1024 neighbouring positions
- valid_frames: int32 [8, 4], P(('tmpl', 'rec'), 'tm'), may hold values from 1024 to 2048
Outputs:
- rec_scores: float32 [8, 16, 512], P(('tmpl', 'rec'))
- template_scores: float32 [512], replicated
The draws below stay inside these ranges and needn't reach their ends.
Inputs may be any that keep to these rules, and one draw needn't show every extreme that they name: `rec_ids`: recording numbers never fall along a group's chain; each recording holds 1 to 1024 frames.
All inputs are finite; a program needn't handle non-finite values.
Results may differ from the reference program's by a relative error of at most 0.0003.
Values may be sent and summed in bfloat16 or wider, within the bound.
A program may use at most 64 MiB of HBM per device.

```python
import math
import jax
import jax.numpy as jnp
import numpy as np
from jax import lax

BINS = 128
FRAMES = 64
TEMPLATES = 512
SLAB = 2048
RECS = 16
GROUPS = 8
TIME = 8192
N_TM = 4


def chosen_rows():
    return 2 * (jnp.arange(GROUPS) * 37 + 2) % TEMPLATES


def drawn_rows():
    return chosen_rows() + 1


def shared_bank(key):
    bank = jnp.clip(jax.random.normal(key, (TEMPLATES, FRAMES, BINS), jnp.float32), -4.0, 4.0)
    signed = jnp.where(bank[chosen_rows()] >= 0.0, 4.0, -4.0)
    return bank.at[chosen_rows()].set(signed)


def draw_templates(key, part):
    bank = shared_bank(key)
    return bank.astype(jnp.bfloat16)


def plant_pair(base, copies, cut_cells, first_at):
    flat_index = jnp.arange(FRAMES * BINS, dtype=jnp.float32).reshape(FRAMES, BINS)
    keep = (flat_index[None, :, :] >= cut_cells[:, None, None]).astype(jnp.float32)
    second_at = first_at + 2 * FRAMES
    base = base.at[:, first_at:first_at + FRAMES, :].set(copies)
    second = copies * keep + base[:, second_at:second_at + FRAMES, :] * (1.0 - keep)
    base = base.at[:, second_at:second_at + FRAMES, :].set(second)
    return base


def plant_copies(base, bank, spread_top):
    width_root = (FRAMES * BINS) ** 0.5
    fraction = jnp.arange(GROUPS, dtype=jnp.float32) / max(GROUPS - 1, 1)
    target = 110.0 + spread_top * fraction
    level = target / (4.0 * width_root)
    copies = bank[chosen_rows()] / 4.0 * level[:, None, None]
    cut_cells = jnp.ceil(2.5 * width_root / (4.0 * level))
    base = plant_pair(base, copies, cut_cells, TIME // 2 + 8)
    drawn_level = 1.7 + 1.3 * fraction
    drawn = bank[drawn_rows()] * drawn_level[:, None, None]
    drawn_cut = jnp.ceil(2.5 * width_root / drawn_level)
    base = plant_pair(base, drawn, drawn_cut, 8)
    return base


def draw_corpus(key, part):
    bank = shared_bank(key)
    key = jax.random.fold_in(key, 7)
    loudness = jax.random.uniform(jax.random.fold_in(key, 11), (GROUPS,), jnp.float32, 0.5, 1.5)
    base = jnp.clip(jax.random.normal(key, (GROUPS, TIME, BINS), jnp.float32), -4.0, 4.0)
    base = base * loudness[:, None, None]
    base = plant_copies(base, bank, 220.0)
    return base.astype(jnp.bfloat16)


def place_ends(drawn, rng, least, largest):
    index_at = [jax.random.randint(jax.random.fold_in(rng, axis), (), 0, length) for axis, length in enumerate(drawn.shape)]
    widest = drawn.shape.index(max(drawn.shape))
    next_to = index_at[:widest] + [(index_at[widest] + 1) % drawn.shape[widest]] + index_at[widest + 1:]
    return drawn.at[tuple(index_at)].set(least).at[tuple(next_to)].set(largest)


def profile(number_of, total, reach, skew):
    portions = [(1 << 20) // math.isqrt(standing ** skew) + 1 for standing in range(2, number_of + 1)]
    surplus, given = total - reach - (number_of - 1), [1] * (number_of - 1)
    while surplus > 0:
        candidates = [i for i in range(number_of - 1) if given[i] < reach]
        pool, budget = sum([portions[i] for i in candidates]), surplus
        for i in candidates:
            addition = min(reach - given[i], max(1, budget * portions[i] // pool), surplus)
            given[i] = given[i] + addition
            surplus = surplus - addition
    return np.array([reach] + given)


def ragged(key, amount, total, reach, lean):
    if amount == 2:
        one = jax.random.randint(key, (), max(1, total - reach), min(reach, total - 1) + 1)
        return jnp.stack([one, total - one])
    sizes = jnp.asarray(profile(amount, total, reach, lean), jnp.int32)
    twos = (amount - 1) // 2
    donor, taker = sizes[1:1 + 2 * twos:2], sizes[2:2 + 2 * twos:2]
    room = jnp.minimum(donor - 1, reach - taker)
    shifted = jax.random.randint(jax.random.fold_in(key, 1), (twos,), 0, 1 << 20) % (room + 1)
    sizes = sizes.at[1:1 + 2 * twos:2].set(donor - shifted).at[2:2 + 2 * twos:2].set(taker + shifted)
    return sizes[jax.random.permutation(jax.random.fold_in(key, 2), amount)]


def setup_inputs(seed: int = 0) -> dict:
    splits = jax.random.split(jax.random.key(seed), 5)
    return {
        "corpus": draw_corpus(jax.random.fold_in(splits[4], 71), 0),
        "templates": draw_templates(jax.random.fold_in(splits[4], 71), 0),
        "rec_ids": jax.vmap(lambda own: jnp.searchsorted(jnp.cumsum(ragged(own, RECS, TIME, 2 * TIME // RECS, 1)), jnp.arange(TIME), side="right"))(jax.random.split(splits[2], GROUPS)).reshape((GROUPS, TIME)).astype(jnp.int32),
        "valid_frames": place_ends(jax.random.randint(splits[3], (GROUPS, N_TM), SLAB // 2, SLAB + 1), jax.random.fold_in(splits[3], 1), SLAB // 2, SLAB).astype(jnp.int32),
    }


def slab_stats(scores, frame_ids, usable_count):
    length = scores.shape[-1]
    margin = frame_ids.shape[0] - length
    positions = jnp.arange(length, dtype=jnp.int32)
    usable = (positions < usable_count) & (frame_ids[margin:] == frame_ids[:length])
    labels = jnp.arange(RECS, dtype=jnp.int32)
    member = ((frame_ids[:length][None, :] == labels[:, None]) & usable[None, :]).astype(jnp.float32)

    def top_of(label_row):
        return jnp.max(jnp.where(label_row[None, :] > 0, scores, -jnp.inf), axis=1)

    peaks = jnp.maximum(lax.map(top_of, member), 0.0)
    spread = jnp.dot(peaks.T, member, precision=lax.Precision.HIGHEST)
    weights = jnp.where(usable[None, :], jnp.exp(scores - spread), 0.0)
    totals = jnp.dot(member, weights.T, precision=lax.Precision.HIGHEST)
    return peaks, totals


def reference(corpus, templates, rec_ids, valid_frames):
    bank = templates.reshape(TEMPLATES, FRAMES * BINS)
    score_scale = (FRAMES * BINS) ** -0.5

    def group_stats(inputs):
        frames_g, ids_g, valid_g = inputs
        padded = jnp.concatenate([frames_g, jnp.zeros((FRAMES - 1, BINS), jnp.bfloat16)], axis=0)
        padded_ids = jnp.concatenate([ids_g, jnp.full((FRAMES - 1,), -1, jnp.int32)], axis=0)

        def slab_part(index):
            begin = (index * SLAB).astype(jnp.int32)
            extended = lax.dynamic_slice_in_dim(padded, begin, SLAB + FRAMES - 1, 0)
            ext_ids = lax.dynamic_slice_in_dim(padded_ids, begin, SLAB + FRAMES - 1, 0)
            unfolded = jnp.stack([extended[lagged:lagged + SLAB] for lagged in range(FRAMES)], axis=1)
            unfolded = unfolded.reshape(SLAB, FRAMES * BINS)
            scores = jnp.dot(bank, unfolded.T, preferred_element_type=jnp.float32) * score_scale
            return slab_stats(scores, ext_ids, valid_g[index])

        peaks, totals = lax.map(slab_part, jnp.arange(N_TM, dtype=jnp.int32))
        best = jnp.max(peaks, axis=0)
        summed = jnp.sum(totals * jnp.exp(peaks - best[None]), axis=0)
        return best, summed

    peaks, totals = lax.map(group_stats, (corpus, rec_ids, valid_frames))
    rec_scores = peaks + jnp.log(jnp.exp(-peaks) + totals)
    top = jnp.max(peaks, axis=(0, 1))
    whole = jnp.sum(totals * jnp.exp(peaks - top[None, None]), axis=(0, 1))
    template_scores = top + jnp.log(jnp.exp(-top) + whole)
    return rec_scores, template_scores
```

```python
import functools

import jax
import jax.numpy as jnp
from jax import lax
from jax.experimental import pallas as pl
from jax.experimental.pallas import tpu as pltpu
from jax.sharding import PartitionSpec as P

RECS = 16
SHIFTS = 16
ROWS = 512
PIECE = 64
LOW = -1e30
MESH = pl.DeviceIdType.MESH


def kernel(
    n, n_tm, score_scale,
    corpus, bank, meta, rec_out, top_out,
    frames, wide, unfolded, weights, scores, ids, rim_ids, bias, labels,
    piece_max, piece_sum, stats, slabs, group, groups_all,
    local_sem, send_sem, recv_sem,
):
    i, z, c = lax.axis_index("tmpl"), lax.axis_index("tm"), lax.axis_index("rec")
    parity = lax.rem(i, 2)
    side = i + 1 - 2 * parity
    rows = bank.shape[0]
    length = corpus.shape[0]
    halo = frames.shape[1] - length
    chunks = weights.shape[0]
    depth = weights.shape[2]
    cols = weights.shape[1]
    id_rows = length // 128
    half = n // 2

    def at(j, zz, cc):
        return {"tmpl": j, "tm": zz, "rec": cc}

    def tmpl_plus(by):
        return lax.rem(i + by + n, n)

    def tm_plus(by):
        return lax.rem(z + by + n_tm, n_tm)

    slots = {}

    def slot(name):
        return slots.setdefault(name, len(slots))

    def remote(name, src, dst, device):
        k = slot(name)
        return pltpu.make_async_remote_copy(
            src_ref=src, dst_ref=dst, send_sem=send_sem.at[k], recv_sem=recv_sem.at[k],
            device_id=device, device_id_type=MESH,
        )

    def block(q, j, cc):
        shard = (j // 2) * 2 + cc
        return weights.at[q, pl.ds(pl.multiple_of(shard * rows, 16), rows)]

    own_frames = pltpu.make_async_copy(corpus, frames.at[0, pl.ds(0, length)], local_sem.at[0])
    own_meta = pltpu.make_async_copy(meta, ids.at[0], local_sem.at[1])
    own_frames.start()
    own_meta.start()
    own_bank = []
    for q in range(chunks):
        own_bank.append(pltpu.make_async_copy(
            bank.at[:, pl.ds(q * depth, depth)], block(q, i, c), local_sem.at[2 + q]))
        own_bank[-1].start()

    barrier = pltpu.get_barrier_semaphore()
    partners = [at(tmpl_plus(dj), z, c if dc == 0 else 1 - c)
                for dj in range(n) for dc in range(2) if dj or dc]
    for dz in range(1, n_tm):
        partners += [at(i, tm_plus(dz), c), at(side, tm_plus(dz), c)]
    for device in partners:
        pl.semaphore_signal(barrier, inc=1, device_id=device, device_id_type=MESH)
    pl.semaphore_wait(barrier, len(partners))

    sent = []

    def start(copy):
        copy.start()
        sent.append(copy)

    rim = corpus.at[pl.ds(0, halo)]
    rim_meta = meta.at[pl.ds(0, 8)]
    before, after = tm_plus(-1), tm_plus(1)
    rim_copies = []
    for g, j in ((0, i), (1, side)):
        rim_copies.append(remote(("rim", g), rim, frames.at[g, pl.ds(length, halo)], at(j, before, c)))
        rim_copies.append(remote(("rim_ids", g), rim_meta, rim_ids.at[g], at(j, before, c)))

    @pl.when(z > 0)
    def _():
        for copy in rim_copies:
            copy.start()

    @pl.when(z == n_tm - 1)
    def _():
        for g in range(2):
            frames[g, pl.ds(length, halo), :] = jnp.zeros((halo, frames.shape[2]), jnp.bfloat16)
            rim_ids[g] = jnp.full(rim_ids.shape[1:], -1, jnp.int32)

    side_meta = remote("meta", meta, ids.at[1], at(side, z, c))
    start(side_meta)
    side_frames = remote("frames", corpus, frames.at[1, pl.ds(0, length)], at(side, z, c))
    for q in range(chunks):
        part = bank.at[:, pl.ds(q * depth, depth)]
        for d in range(1, half):
            start(remote(("bank", q, d), part, block(q, i, c), at(tmpl_plus(2 * d), z, c)))
        start(remote(("core", q), part, block(q, i, c), at(i, z, 1 - c)))
        if q == 0:
            start(side_frames)

    def arrive_bank(q):
        for d in range(1, half):
            j = tmpl_plus(-2 * d)
            remote(("bank", q, d), block(q, j, c), block(q, j, c), at(j, z, c)).wait_recv()
            start(remote(("pass", q, d), block(q, j, c), block(q, j, c), at(i, z, 1 - c)))

    def finish_bank(q):
        own_bank[q].wait()
        here = block(q, i, 1 - c)
        remote(("core", q), here, here, at(i, z, 1 - c)).wait_recv()
        for d in range(1, half):
            there = block(q, tmpl_plus(-2 * d), 1 - c)
            remote(("pass", q, d), there, there, at(i, z, 1 - c)).wait_recv()

    def unfold(g):
        @pl.when(z < n_tm - 1)
        def _():
            rim_copies[2 * g].wait_recv()
            rim_copies[2 * g + 1].wait_recv()

        total = length + halo
        wide[pl.ds(total, SHIFTS), :] = jnp.zeros((SHIFTS, wide.shape[1]), jnp.float32)

        @pl.loop(0, total // 64)
        def _(step):
            here = pl.ds(pl.multiple_of(step * 64, 64), 64)
            wide[here, :] = frames[g, here, :].astype(jnp.float32)

        @pl.loop(0, total // 64)
        def _(step):
            base = pl.multiple_of(step * 64, 64)
            for s in range(SHIFTS):
                unfolded[g, pl.ds(base, 64), s * 128:(s + 1) * 128] = (
                    wide[pl.ds(base + s, 64), :].astype(jnp.bfloat16))

        now = ids[g, 0:id_rows, :]
        rolled = pltpu.roll(now, 128 - (PIECE - 1), 1)
        rolled_rim = pltpu.roll(rim_ids[g], 128 - (PIECE - 1), 1)
        next_row = jnp.concatenate([rolled[1:], rolled_rim[0:1]], axis=0)
        lane = lax.broadcasted_iota(jnp.int32, now.shape, 1)
        row = lax.broadcasted_iota(jnp.int32, now.shape, 0)
        last = jnp.where(lane < 128 - (PIECE - 1), rolled, next_row)
        valid = ids[g, id_rows:id_rows + 1, :]
        usable = (now == last) & (row * 128 + lane < valid)
        flat = jnp.where(usable, 0.0, LOW)
        flat = jnp.concatenate([flat, jnp.zeros((128 - id_rows, 128), jnp.float32)], axis=0)
        turned = flat.T
        for r in range(id_rows):
            bias[g, r * 128:(r + 1) * 128, :] = jnp.broadcast_to(turned[:, r:r + 1], (128, 128))
        named = jnp.where(usable, now, -1)
        first = jnp.max(jnp.where(lane < PIECE, named, -1), axis=1, keepdims=True)
        second = jnp.max(jnp.where(lane >= PIECE, named, -1), axis=1, keepdims=True)
        labels[g, 0:id_rows, :] = jnp.broadcast_to(first, (id_rows, 128))
        labels[g, id_rows:2 * id_rows, :] = jnp.broadcast_to(second, (id_rows, 128))

    def correlate(g, q):
        @pl.loop(0, length // ROWS)
        def _(step):
            base = pl.multiple_of(step * ROWS, ROWS)
            part = lax.dot_general(
                unfolded[g, pl.ds(pl.multiple_of(base + q * SHIFTS, SHIFTS), ROWS), :], weights[q],
                (((1,), (1,)), ((), ())), preferred_element_type=jnp.float32)
            if q == 0:
                scores[g, pl.ds(base, ROWS), :] = part
            else:
                scores[g, pl.ds(base, ROWS), :] += part

    def summarize(g):
        @pl.loop(0, id_rows)
        def _(r):
            for h in range(2):
                base = pl.multiple_of(r * 128 + h * PIECE, PIECE)
                mask = bias[g, pl.ds(base, PIECE), :]
                for k in range(0, cols, 128):
                    x = scores[g, pl.ds(base, PIECE), k:k + 128] * score_scale + mask
                    top = jnp.maximum(jnp.max(x, axis=0, keepdims=True), 0.0)
                    piece_max[k // 128, pl.ds(h * id_rows + r, 1), :] = top
                    piece_sum[k // 128, pl.ds(h * id_rows + r, 1), :] = jnp.sum(
                        jnp.exp(x - top), axis=0, keepdims=True)

        name = jnp.concatenate([labels[g]] * (cols // 128), axis=1)
        tops = jnp.concatenate([piece_max[k] for k in range(cols // 128)], axis=1)
        sums = jnp.concatenate([piece_sum[k] for k in range(cols // 128)], axis=1)
        for r in range(RECS):
            mine = name == r
            peak = jnp.max(jnp.where(mine, tops, 0.0), axis=0, keepdims=True)
            total = jnp.sum(jnp.where(mine, sums * jnp.exp(jnp.minimum(tops - peak, 0.0)), 0.0), axis=0, keepdims=True)
            stats[g, r:r + 1, :] = peak
            stats[g, RECS + r:RECS + r + 1, :] = total

    own_frames.wait()
    own_meta.wait()
    unfold(0)
    arrive_bank(0)
    finish_bank(0)
    for q in range(chunks - 1):
        correlate(0, q)
        arrive_bank(q + 1)
        if q == 0:
            side_frames.wait_recv()
            side_meta.wait_recv()
            unfold(1)
        correlate(1, q)
        finish_bank(q + 1)
    correlate(1, chunks - 1)
    summarize(1)
    for dz in range(n_tm):
        start(remote(("side", dz), stats.at[1], slabs.at[z, parity], at(side, tm_plus(dz), c)))
    correlate(0, chunks - 1)
    summarize(0)
    for dz in range(1, n_tm):
        start(remote(("own", dz), stats.at[0], slabs.at[z, parity], at(i, tm_plus(dz), c)))
    slabs[z, parity] = stats[0]
    for dz in range(n_tm):
        there = slabs.at[tm_plus(-dz), 1 - parity]
        remote(("side", dz), there, there, at(side, z, c)).wait_recv()
    for dz in range(1, n_tm):
        there = slabs.at[tm_plus(-dz), parity]
        remote(("own", dz), there, there, at(i, tm_plus(-dz), c)).wait_recv()

    for h in range(2):
        peak = slabs[0, h, 0:RECS, :]
        for s in range(1, n_tm):
            peak = jnp.maximum(peak, slabs[s, h, 0:RECS, :])
        total = jnp.zeros_like(peak)
        for s in range(n_tm):
            total += slabs[s, h, RECS:2 * RECS, :] * jnp.exp(slabs[s, h, 0:RECS, :] - peak)
        rec_out[h] = peak + jnp.log(jnp.exp(-peak) + total)
        top = jnp.max(peak, axis=0, keepdims=True)
        group[2 * h:2 * h + 1, :] = top
        group[2 * h + 1:2 * h + 2, :] = jnp.sum(total * jnp.exp(peak - top), axis=0, keepdims=True)
    group[4:8, :] = jnp.zeros((4, cols), jnp.float32)

    mine = 2 * i + c
    for dj in range(n):
        for dc in range(2):
            if dj or dc:
                start(remote(("group", dj, dc), group, groups_all.at[mine],
                             at(tmpl_plus(dj), z, c if dc == 0 else 1 - c)))
    groups_all[mine] = group[...]
    for dj in range(n):
        for dc in range(2):
            if dj or dc:
                there = groups_all.at[2 * tmpl_plus(-dj) + (c if dc == 0 else 1 - c)]
                remote(("group", dj, dc), there, there, at(tmpl_plus(-dj), z, c if dc == 0 else 1 - c)).wait_recv()
    for h in range(2):
        top = groups_all[0, 2 * h:2 * h + 1, :]
        for s in range(1, 2 * n):
            top = jnp.maximum(top, groups_all[s, 2 * h:2 * h + 1, :])
        total = jnp.zeros_like(top)
        for s in range(2 * n):
            total += groups_all[s, 2 * h + 1:2 * h + 2, :] * jnp.exp(groups_all[s, 2 * h:2 * h + 1, :] - top)
        top_out[h:h + 1, :] = top + jnp.log(jnp.exp(-top) + total)

    for copy in sent:
        copy.wait_send()

    @pl.when(z > 0)
    def _():
        for copy in rim_copies:
            copy.wait_send()


def on_device(n, n_tm, corpus, templates, rec_ids, valid_frames):
    rows, span, bins = templates.shape
    length = corpus.shape[1]
    halo = span
    id_rows = length // 128
    chunks = span // SHIFTS
    depth = SHIFTS * bins
    cols = rows * n
    meta = jnp.concatenate(
        [rec_ids.reshape(id_rows, 128), jnp.broadcast_to(valid_frames.reshape(1, 1), (8, 128))], axis=0)
    copies = 5 + chunks * n + 2 * n_tm + 2 * n
    f32, bf16, i32 = jnp.float32, jnp.bfloat16, jnp.int32
    rec_half, top_half = pl.pallas_call(
        functools.partial(kernel, n, n_tm, (span * bins) ** (-0.5)),
        out_shape=(jax.ShapeDtypeStruct((2, RECS, cols), f32), jax.ShapeDtypeStruct((2, cols), f32)),
        in_specs=[pl.BlockSpec(memory_space=pl.ANY)] * 3,
        out_specs=(pl.BlockSpec(memory_space=pltpu.VMEM), pl.BlockSpec(memory_space=pltpu.VMEM)),
        scratch_shapes=[
            pltpu.VMEM((2, length + halo, bins), bf16),
            pltpu.VMEM((length + halo + SHIFTS, bins), f32),
            pltpu.VMEM((2, length + halo, depth), bf16),
            pltpu.VMEM((chunks, cols, depth), bf16),
            pltpu.VMEM((2, length, cols), f32),
            pltpu.VMEM((2, id_rows + 8, 128), i32),
            pltpu.VMEM((2, 8, 128), i32),
            pltpu.VMEM((2, length, 128), f32),
            pltpu.VMEM((2, 2 * id_rows, 128), i32),
            pltpu.VMEM((cols // 128, 2 * id_rows, 128), f32),
            pltpu.VMEM((cols // 128, 2 * id_rows, 128), f32),
            pltpu.VMEM((2, 2 * RECS, cols), f32),
            pltpu.VMEM((n_tm, 2, 2 * RECS, cols), f32),
            pltpu.VMEM((8, cols), f32),
            pltpu.VMEM((2 * n, 8, cols), f32),
            pltpu.SemaphoreType.DMA((2 + chunks,)),
            pltpu.SemaphoreType.DMA((copies,)),
            pltpu.SemaphoreType.DMA((copies,)),
        ],
        compiler_params=pltpu.CompilerParams(
            collective_id=0, has_side_effects=True, vmem_limit_bytes=48 * 1024 * 1024),
    )(corpus[0], templates.reshape(rows, span * bins), meta)
    rec = rec_half.reshape(2, RECS, n // 2, 2 * rows).transpose(1, 2, 0, 3).reshape(1, RECS, n * 2 * rows)
    top = top_half.reshape(2, n // 2, 2 * rows).transpose(1, 0, 2).reshape(n * 2 * rows)
    return rec, top


def solution(mesh):
    return jax.shard_map(
        functools.partial(on_device, mesh.shape["tmpl"], mesh.shape["tm"]),
        mesh=mesh,
        in_specs=(
            P(("tmpl", "rec"), "tm", None),
            P(("tmpl", "rec"), None, None),
            P(("tmpl", "rec"), "tm"),
            P(("tmpl", "rec"), "tm"),
        ),
        out_specs=(P(("tmpl", "rec"), None, None), P()),
        check_vma=False,
    )
```

```python
import functools

import jax
import jax.numpy as jnp
from jax import lax
from jax.experimental import pallas as pl
from jax.experimental.pallas import tpu as pltpu
from jax.sharding import PartitionSpec as P

RECS = 16
SHIFTS = 16
HALF = 8
ROWS = 1024
PIECE = 64
LOW = -1e30
MESH = pl.DeviceIdType.MESH


def kernel(
    n, n_tm, score_scale,
    corpus, bank, meta, rec_out, top_out,
    frames, wide, unfolded, weights, scores, ids, rim_ids, bias, labels,
    piece_max, piece_sum, stats, slabs, group, groups_all,
    local_sem, send_sem, recv_sem,
):
    i, z, c = lax.axis_index("tmpl"), lax.axis_index("tm"), lax.axis_index("rec")
    parity = lax.rem(i, 2)
    side = i + 1 - 2 * parity
    rows = bank.shape[0]
    length = corpus.shape[0]
    halo = frames.shape[1] - length
    chunks = weights.shape[0]
    depth = weights.shape[2]
    cols = weights.shape[1]
    id_rows = length // 128
    half = n // 2
    near = z + 1 - 2 * lax.rem(z, 2)
    mine_half = lax.rem(z, 2)

    def at(j, zz, cc):
        return {"tmpl": j, "tm": zz, "rec": cc}

    def tmpl_plus(by):
        return lax.rem(i + by + n, n)

    def tm_plus(by):
        return lax.rem(z + by + n_tm, n_tm)

    slots = {}

    def slot(name):
        return slots.setdefault(name, len(slots))

    def remote(name, src, dst, device):
        k = slot(name)
        return pltpu.make_async_remote_copy(
            src_ref=src, dst_ref=dst, send_sem=send_sem.at[k], recv_sem=recv_sem.at[k],
            device_id=device, device_id_type=MESH,
        )

    def block(q, j, cc):
        shard = (j // 2) * 2 + cc
        return weights.at[q, pl.ds(pl.multiple_of(shard * rows, 16), rows)]

    def half_block(q, j, cc, which):
        first = ((j // 2) * 2 + cc) * rows + which * (rows // 2)
        return weights.at[q, pl.ds(pl.multiple_of(first, 16), rows // 2)]

    own_frames = pltpu.make_async_copy(corpus, frames.at[0, pl.ds(0, length)], local_sem.at[0])
    own_meta = pltpu.make_async_copy(meta, ids.at[0], local_sem.at[1])
    own_frames.start()
    own_meta.start()
    own_bank = []
    for q in range(chunks):
        own_bank.append(pltpu.make_async_copy(
            bank.at[:, pl.ds(q * depth, depth)], block(q, i, c), local_sem.at[2 + q]))
        own_bank[-1].start()

    barrier = pltpu.get_barrier_semaphore()
    partners = [at(tmpl_plus(dj), z, c if dc == 0 else 1 - c)
                for dj in range(n) for dc in range(2) if dj or dc]
    for dz in range(1, n_tm):
        partners += [at(i, tm_plus(dz), c), at(side, tm_plus(dz), c)]
    for device in partners:
        pl.semaphore_signal(barrier, inc=1, device_id=device, device_id_type=MESH)
    pl.semaphore_wait(barrier, len(partners))

    sent = []

    def start(copy):
        copy.start()
        sent.append(copy)

    rim = corpus.at[pl.ds(0, halo)]
    rim_meta = meta.at[pl.ds(0, 8)]
    before, after = tm_plus(-1), tm_plus(1)
    rim_copies = []
    for g, j in ((0, i), (1, side)):
        rim_copies.append(remote(("rim", g), rim, frames.at[g, pl.ds(length, halo)], at(j, before, c)))
        rim_copies.append(remote(("rim_ids", g), rim_meta, rim_ids.at[g], at(j, before, c)))

    @pl.when(z > 0)
    def _():
        for copy in rim_copies:
            copy.start()

    @pl.when(z == n_tm - 1)
    def _():
        for g in range(2):
            frames[g, pl.ds(length, halo), :] = jnp.zeros((halo, frames.shape[2]), jnp.bfloat16)
            rim_ids[g] = jnp.full(rim_ids.shape[1:], -1, jnp.int32)

    side_meta = remote("meta", meta, ids.at[1], at(side, z, c))
    start(side_meta)
    side_frames = remote("frames", corpus, frames.at[1, pl.ds(0, length)], at(side, z, c))
    for q in range(chunks):
        own_half = bank.at[pl.ds(pl.multiple_of(mine_half * (rows // 2), 16), rows // 2), pl.ds(q * depth, depth)]
        for d in range(1, half):
            start(remote(("bank", q, d), own_half, half_block(q, i, c, mine_half), at(tmpl_plus(2 * d), z, c)))
        start(remote(("core", q), bank.at[:, pl.ds(q * depth, depth)], block(q, i, c), at(i, z, 1 - c)))
        if q == 0:
            start(side_frames)

    def arrive(q):
        if q >= chunks:
            return
        for d in range(1, half):
            there = half_block(q, tmpl_plus(-2 * d), c, mine_half)
            remote(("bank", q, d), there, there, at(i, near, c)).wait_recv()
            start(remote(("near", q, d), there, there, at(i, near, c)))
            start(remote(("pass", q, d, 0), there, there, at(i, z, 1 - c)))

    def arrive_near(q):
        if q >= chunks:
            return
        for d in range(1, half):
            there = half_block(q, tmpl_plus(-2 * d), c, 1 - mine_half)
            remote(("near", q, d), there, there, at(i, near, c)).wait_recv()
            start(remote(("pass", q, d, 1), there, there, at(i, z, 1 - c)))

    def finish(q):
        own_bank[q].wait()
        here = block(q, i, 1 - c)
        remote(("core", q), here, here, at(i, z, 1 - c)).wait_recv()
        for d in range(1, half):
            for k, which in ((0, mine_half), (1, 1 - mine_half)):
                there = half_block(q, tmpl_plus(-2 * d), 1 - c, which)
                remote(("pass", q, d, k), there, there, at(i, z, 1 - c)).wait_recv()

    def unfold(g):
        @pl.when(z < n_tm - 1)
        def _():
            rim_copies[2 * g].wait_recv()
            rim_copies[2 * g + 1].wait_recv()

        total = length + halo
        wide[pl.ds(total, SHIFTS), :] = jnp.zeros((SHIFTS, wide.shape[1]), jnp.float32)

        @pl.loop(0, total // 64)
        def _(step):
            here = pl.ds(pl.multiple_of(step * 64, 64), 64)
            wide[here, :] = frames[g, here, :].astype(jnp.float32)

        @pl.loop(0, total // 64)
        def _(step):
            base = pl.multiple_of(step * 64, 64)
            for s in range(SHIFTS):
                unfolded[g, pl.ds(base, 64), s * 128:(s + 1) * 128] = (
                    wide[pl.ds(base + s, 64), :].astype(jnp.bfloat16))

        now = ids[g, 0:id_rows, :]
        rolled = pltpu.roll(now, 128 - (PIECE - 1), 1)
        rolled_rim = pltpu.roll(rim_ids[g], 128 - (PIECE - 1), 1)
        next_row = jnp.concatenate([rolled[1:], rolled_rim[0:1]], axis=0)
        lane = lax.broadcasted_iota(jnp.int32, now.shape, 1)
        row = lax.broadcasted_iota(jnp.int32, now.shape, 0)
        last = jnp.where(lane < 128 - (PIECE - 1), rolled, next_row)
        valid = ids[g, id_rows:id_rows + 1, :]
        usable = (now == last) & (row * 128 + lane < valid)
        flat = jnp.where(usable, 0.0, LOW)
        flat = jnp.concatenate([flat, jnp.zeros((128 - id_rows, 128), jnp.float32)], axis=0)
        turned = flat.T
        for r in range(id_rows):
            bias[g, r * 128:(r + 1) * 128, :] = jnp.broadcast_to(turned[:, r:r + 1], (128, 128))
        named = jnp.where(usable, now, -1)
        first = jnp.max(jnp.where(lane < PIECE, named, -1), axis=1, keepdims=True)
        second = jnp.max(jnp.where(lane >= PIECE, named, -1), axis=1, keepdims=True)
        labels[g, 0:id_rows, :] = jnp.broadcast_to(first, (id_rows, 128))
        labels[g, id_rows:2 * id_rows, :] = jnp.broadcast_to(second, (id_rows, 128))

    def correlate(q):
        first = q * HALF // SHIFTS * SHIFTS
        lanes = slice(q * depth % unfolded.shape[2], q * depth % unfolded.shape[2] + depth)
        part = lax.dot_general(
            unfolded[0, first:first + length, lanes], weights[q],
            (((1,), (1,)), ((), ())), preferred_element_type=jnp.float32)
        if q == 0:
            scores[0] = part
        else:
            scores[0] += part

    def correlate_all(g):
        @pl.loop(0, length // ROWS)
        def _(step):
            base = pl.multiple_of(step * ROWS, ROWS)
            total = None
            for q in range(chunks):
                first = q * HALF // SHIFTS * SHIFTS
                lanes = slice(q * depth % unfolded.shape[2], q * depth % unfolded.shape[2] + depth)
                part = lax.dot_general(
                    unfolded[g, pl.ds(pl.multiple_of(base + first, SHIFTS), ROWS), lanes], weights[q],
                    (((1,), (1,)), ((), ())), preferred_element_type=jnp.float32)
                total = part if total is None else total + part
            scores[g, pl.ds(base, ROWS), :] = total

    def log_of(peak, total):
        return jnp.where(total > 0.0, peak + jnp.log(total), LOW)

    def summarize(g):
        @pl.loop(0, id_rows)
        def _(r):
            for h in range(2):
                base = pl.multiple_of(r * 128 + h * PIECE, PIECE)
                mask = bias[g, pl.ds(base, PIECE), :]
                for k in range(0, cols, 128):
                    x = scores[g, pl.ds(base, PIECE), k:k + 128] * score_scale + mask
                    top = jnp.maximum(jnp.max(x, axis=0, keepdims=True), 0.0)
                    piece_max[k // 128, pl.ds(h * id_rows + r, 1), :] = top
                    piece_sum[k // 128, pl.ds(h * id_rows + r, 1), :] = jnp.sum(
                        jnp.exp(x - top), axis=0, keepdims=True)

        name = jnp.concatenate([labels[g]] * (cols // 128), axis=1)
        tops = jnp.concatenate([piece_max[k] for k in range(cols // 128)], axis=1)
        sums = jnp.concatenate([piece_sum[k] for k in range(cols // 128)], axis=1)
        for r in range(RECS):
            mine = name == r
            peak = jnp.max(jnp.where(mine, tops, 0.0), axis=0, keepdims=True)
            total = jnp.sum(jnp.where(mine, sums * jnp.exp(jnp.minimum(tops - peak, 0.0)), 0.0), axis=0, keepdims=True)
            stats[g, r:r + 1, :] = log_of(peak, total)

    own_frames.wait()
    own_meta.wait()
    unfold(0)
    arrive(0)
    arrive(1)
    arrive_near(0)
    arrive(2)
    arrive_near(1)
    finish(0)
    for q in range(chunks):
        correlate(q)
        arrive(q + 3)
        arrive_near(q + 2)
        if q + 1 < chunks:
            finish(q + 1)
    summarize(0)
    for dz in range(1, n_tm):
        start(remote(("own", dz), stats.at[0], slabs.at[z, parity], at(i, tm_plus(dz), c)))
    side_frames.wait_recv()
    side_meta.wait_recv()
    unfold(1)
    correlate_all(1)
    summarize(1)
    for dz in range(n_tm):
        start(remote(("side", dz), stats.at[1], slabs.at[z, parity], at(side, tm_plus(dz), c)))
    slabs[z, parity] = stats[0]
    for dz in range(n_tm):
        there = slabs.at[tm_plus(-dz), 1 - parity]
        remote(("side", dz), there, there, at(side, z, c)).wait_recv()
    for dz in range(1, n_tm):
        there = slabs.at[tm_plus(-dz), parity]
        remote(("own", dz), there, there, at(i, tm_plus(-dz), c)).wait_recv()

    for h in range(2):
        peak = jnp.maximum(slabs[0, h], 0.0)
        for s in range(1, n_tm):
            peak = jnp.maximum(peak, slabs[s, h])
        total = jnp.zeros_like(peak)
        for s in range(n_tm):
            total += jnp.exp(slabs[s, h] - peak)
        rec_out[h] = peak + jnp.log(jnp.exp(-peak) + total)
        top = jnp.max(peak, axis=0, keepdims=True)
        group[h:h + 1, :] = log_of(top, jnp.sum(total * jnp.exp(peak - top), axis=0, keepdims=True))
    group[2:8, :] = jnp.zeros((6, cols), jnp.float32)

    mine = 2 * i + c
    for dj in range(n):
        for dc in range(2):
            if dj or dc:
                start(remote(("group", dj, dc), group, groups_all.at[mine],
                             at(tmpl_plus(dj), z, c if dc == 0 else 1 - c)))
    groups_all[mine] = group[...]
    for dj in range(n):
        for dc in range(2):
            if dj or dc:
                there = groups_all.at[2 * tmpl_plus(-dj) + (c if dc == 0 else 1 - c)]
                remote(("group", dj, dc), there, there, at(tmpl_plus(-dj), z, c if dc == 0 else 1 - c)).wait_recv()
    top = jnp.maximum(groups_all[0, 0:2, :], 0.0)
    for s in range(1, 2 * n):
        top = jnp.maximum(top, groups_all[s, 0:2, :])
    total = jnp.zeros_like(top)
    for s in range(2 * n):
        total += jnp.exp(groups_all[s, 0:2, :] - top)
    top_out[...] = top + jnp.log(jnp.exp(-top) + total)

    for copy in sent:
        copy.wait_send()

    @pl.when(z > 0)
    def _():
        for copy in rim_copies:
            copy.wait_send()


def on_device(n, n_tm, corpus, templates, rec_ids, valid_frames):
    rows, span, bins = templates.shape
    length = corpus.shape[1]
    halo = span
    id_rows = length // 128
    chunks = span // HALF
    depth = HALF * bins
    cols = rows * n
    meta = jnp.concatenate(
        [rec_ids.reshape(id_rows, 128), jnp.broadcast_to(valid_frames.reshape(1, 1), (8, 128))], axis=0)
    copies = 6 + chunks * 2 * n + 2 * n_tm + 2 * n
    f32, bf16, i32 = jnp.float32, jnp.bfloat16, jnp.int32
    rec_half, top_half = pl.pallas_call(
        functools.partial(kernel, n, n_tm, (span * bins) ** (-0.5)),
        out_shape=(jax.ShapeDtypeStruct((2, RECS, cols), f32), jax.ShapeDtypeStruct((2, cols), f32)),
        in_specs=[pl.BlockSpec(memory_space=pl.ANY)] * 3,
        out_specs=(pl.BlockSpec(memory_space=pltpu.VMEM), pl.BlockSpec(memory_space=pltpu.VMEM)),
        scratch_shapes=[
            pltpu.VMEM((2, length + halo, bins), bf16),
            pltpu.VMEM((length + halo + SHIFTS, bins), f32),
            pltpu.VMEM((2, length + halo, SHIFTS * bins), bf16),
            pltpu.VMEM((chunks, cols, depth), bf16),
            pltpu.VMEM((2, length, cols), f32),
            pltpu.VMEM((2, id_rows + 8, 128), i32),
            pltpu.VMEM((2, 8, 128), i32),
            pltpu.VMEM((2, length, 128), f32),
            pltpu.VMEM((2, 2 * id_rows, 128), i32),
            pltpu.VMEM((cols // 128, 2 * id_rows, 128), f32),
            pltpu.VMEM((cols // 128, 2 * id_rows, 128), f32),
            pltpu.VMEM((2, RECS, cols), f32),
            pltpu.VMEM((n_tm, 2, RECS, cols), f32),
            pltpu.VMEM((8, cols), f32),
            pltpu.VMEM((2 * n, 8, cols), f32),
            pltpu.SemaphoreType.DMA((2 + chunks,)),
            pltpu.SemaphoreType.DMA((copies,)),
            pltpu.SemaphoreType.DMA((copies,)),
        ],
        compiler_params=pltpu.CompilerParams(
            collective_id=0, has_side_effects=True, vmem_limit_bytes=48 * 1024 * 1024),
    )(corpus[0], templates.reshape(rows, span * bins), meta)
    rec = rec_half.reshape(2, RECS, n // 2, 2 * rows).transpose(1, 2, 0, 3).reshape(1, RECS, n * 2 * rows)
    top = top_half.reshape(2, n // 2, 2 * rows).transpose(1, 0, 2).reshape(n * 2 * rows)
    return rec, top


def solution(mesh):
    return jax.shard_map(
        functools.partial(on_device, mesh.shape["tmpl"], mesh.shape["tm"]),
        mesh=mesh,
        in_specs=(
            P(("tmpl", "rec"), "tm", None),
            P(("tmpl", "rec"), None, None),
            P(("tmpl", "rec"), "tm"),
            P(("tmpl", "rec"), "tm"),
        ),
        out_specs=(P(("tmpl", "rec"), None, None), P()),
        check_vma=False,
    )
```

```python
import functools

import jax
import jax.numpy as jnp
from jax import lax
from jax.experimental import pallas as pl
from jax.experimental.pallas import tpu as pltpu
from jax.sharding import PartitionSpec as P

RECS = 16
SHIFTS = 16
HALF = 8
ROWS = 1024
PIECE = 64
LOW = -1e30
MESH = pl.DeviceIdType.MESH


def kernel(
    n, n_tm, score_scale,
    corpus, bank, meta, rec_out, top_out,
    frames, wide, unfolded, weights, scores, ids, rim_ids, bias, labels,
    piece_max, piece_sum, stats, slabs, group, groups_all,
    local_sem, send_sem, recv_sem,
):
    i, z, c = lax.axis_index("tmpl"), lax.axis_index("tm"), lax.axis_index("rec")
    parity = lax.rem(i, 2)
    side = i + 1 - 2 * parity
    rows = bank.shape[0]
    length = corpus.shape[0]
    halo = frames.shape[1] - length
    chunks = weights.shape[0]
    depth = weights.shape[2]
    cols = weights.shape[1]
    id_rows = length // 128
    half = n // 2

    def at(j, zz, cc):
        return {"tmpl": j, "tm": zz, "rec": cc}

    def tmpl_plus(by):
        return lax.rem(i + by + n, n)

    def tm_plus(by):
        return lax.rem(z + by + n_tm, n_tm)

    slots = {}

    def slot(name):
        return slots.setdefault(name, len(slots))

    def remote(name, src, dst, device):
        k = slot(name)
        return pltpu.make_async_remote_copy(
            src_ref=src, dst_ref=dst, send_sem=send_sem.at[k], recv_sem=recv_sem.at[k],
            device_id=device, device_id_type=MESH,
        )

    def block(q, j, cc):
        shard = (j // 2) * 2 + cc
        return weights.at[q, pl.ds(pl.multiple_of(shard * rows, 16), rows)]

    barrier = pltpu.get_barrier_semaphore()
    partners = [at(tmpl_plus(dj), z, c if dc == 0 else 1 - c)
                for dj in range(n) for dc in range(2) if dj or dc]
    for dz in range(1, n_tm):
        partners += [at(i, tm_plus(dz), c), at(side, tm_plus(dz), c)]
    for device in partners:
        pl.semaphore_signal(barrier, inc=1, device_id=device, device_id_type=MESH)

    own_frames = pltpu.make_async_copy(corpus, frames.at[0, pl.ds(0, length)], local_sem.at[0])
    own_meta = pltpu.make_async_copy(meta, ids.at[0], local_sem.at[1])
    own_frames.start()
    own_meta.start()
    own_bank = []
    for q in range(chunks):
        own_bank.append(pltpu.make_async_copy(
            bank.at[:, pl.ds(q * depth, depth)], block(q, i, c), local_sem.at[2 + q]))
        own_bank[-1].start()

    pl.semaphore_wait(barrier, len(partners))

    sent = []

    def start(copy):
        copy.start()
        sent.append(copy)

    rim = corpus.at[pl.ds(0, halo)]
    rim_meta = meta.at[pl.ds(0, 8)]
    before, after = tm_plus(-1), tm_plus(1)
    rim_copies = []
    for g, j in ((0, i), (1, side)):
        rim_copies.append(remote(("rim", g), rim, frames.at[g, pl.ds(length, halo)], at(j, before, c)))
        rim_copies.append(remote(("rim_ids", g), rim_meta, rim_ids.at[g], at(j, before, c)))

    @pl.when(z > 0)
    def _():
        for copy in rim_copies:
            copy.start()

    @pl.when(z == n_tm - 1)
    def _():
        for g in range(2):
            frames[g, pl.ds(length, halo), :] = jnp.zeros((halo, frames.shape[2]), jnp.bfloat16)
            rim_ids[g] = jnp.full(rim_ids.shape[1:], -1, jnp.int32)

    side_meta = remote("meta", meta, ids.at[1], at(side, z, c))
    start(side_meta)
    side_frames = remote("frames", corpus, frames.at[1, pl.ds(0, length)], at(side, z, c))
    def send_bank(q):
        if q >= chunks:
            return
        part = bank.at[:, pl.ds(q * depth, depth)]
        for d in range(1, half):
            start(remote(("bank", q, d), part, block(q, i, c), at(tmpl_plus(2 * d), z, c)))
        start(remote(("core", q), part, block(q, i, c), at(i, z, 1 - c)))

    send_bank(0)
    send_bank(1)
    start(side_frames)

    def arrive(q):
        if q >= chunks:
            return
        send_bank(q + 2)
        for d in range(1, half):
            there = block(q, tmpl_plus(-2 * d), c)
            remote(("bank", q, d), there, there, at(i, z, 1 - c)).wait_recv()
            start(remote(("pass", q, d), there, there, at(i, z, 1 - c)))

    def finish(q):
        own_bank[q].wait()
        here = block(q, i, 1 - c)
        remote(("core", q), here, here, at(i, z, 1 - c)).wait_recv()
        for d in range(1, half):
            there = block(q, tmpl_plus(-2 * d), 1 - c)
            remote(("pass", q, d), there, there, at(i, z, 1 - c)).wait_recv()

    def unfold(g):
        @pl.when(z < n_tm - 1)
        def _():
            rim_copies[2 * g].wait_recv()
            rim_copies[2 * g + 1].wait_recv()

        total = length + halo
        wide[pl.ds(total, SHIFTS), :] = jnp.zeros((SHIFTS, wide.shape[1]), jnp.float32)

        @pl.loop(0, total // 64)
        def _(step):
            here = pl.ds(pl.multiple_of(step * 64, 64), 64)
            wide[here, :] = frames[g, here, :].astype(jnp.float32)

        @pl.loop(0, total // 64)
        def _(step):
            base = pl.multiple_of(step * 64, 64)
            for s in range(SHIFTS):
                unfolded[g, pl.ds(base, 64), s * 128:(s + 1) * 128] = (
                    wide[pl.ds(base + s, 64), :].astype(jnp.bfloat16))

        now = ids[g, 0:id_rows, :]
        rolled = pltpu.roll(now, 128 - (PIECE - 1), 1)
        rolled_rim = pltpu.roll(rim_ids[g], 128 - (PIECE - 1), 1)
        next_row = jnp.concatenate([rolled[1:], rolled_rim[0:1]], axis=0)
        lane = lax.broadcasted_iota(jnp.int32, now.shape, 1)
        row = lax.broadcasted_iota(jnp.int32, now.shape, 0)
        last = jnp.where(lane < 128 - (PIECE - 1), rolled, next_row)
        valid = ids[g, id_rows:id_rows + 1, :]
        usable = (now == last) & (row * 128 + lane < valid)
        flat = jnp.where(usable, 0.0, LOW)
        flat = jnp.concatenate([flat, jnp.zeros((128 - id_rows, 128), jnp.float32)], axis=0)
        turned = flat.T
        for r in range(id_rows):
            bias[g, r * 128:(r + 1) * 128, :] = jnp.broadcast_to(turned[:, r:r + 1], (128, 128))
        named = jnp.where(usable, now, -1)
        first = jnp.max(jnp.where(lane < PIECE, named, -1), axis=1, keepdims=True)
        second = jnp.max(jnp.where(lane >= PIECE, named, -1), axis=1, keepdims=True)
        labels[g, 0:id_rows, :] = jnp.broadcast_to(first, (id_rows, 128))
        labels[g, id_rows:2 * id_rows, :] = jnp.broadcast_to(second, (id_rows, 128))

    def correlate(g, q):
        first = q * HALF // SHIFTS * SHIFTS
        lanes = slice(q * depth % unfolded.shape[2], q * depth % unfolded.shape[2] + depth)

        @pl.loop(0, length // ROWS)
        def _(step):
            base = pl.multiple_of(step * ROWS, ROWS)
            part = lax.dot_general(
                unfolded[g, pl.ds(pl.multiple_of(base + first, SHIFTS), ROWS), lanes], weights[q],
                (((1,), (1,)), ((), ())), preferred_element_type=jnp.float32)
            if q == 0:
                scores[g, pl.ds(base, ROWS), :] = part
            else:
                scores[g, pl.ds(base, ROWS), :] += part

    def log_of(peak, total):
        return jnp.where(total > 0.0, peak + jnp.log(total), LOW)

    def summarize(g):
        @pl.loop(0, id_rows)
        def _(r):
            for h in range(2):
                base = pl.multiple_of(r * 128 + h * PIECE, PIECE)
                mask = bias[g, pl.ds(base, PIECE), :]
                for k in range(0, cols, 128):
                    x = scores[g, pl.ds(base, PIECE), k:k + 128] * score_scale + mask
                    top = jnp.maximum(jnp.max(x, axis=0, keepdims=True), 0.0)
                    piece_max[k // 128, pl.ds(h * id_rows + r, 1), :] = top
                    piece_sum[k // 128, pl.ds(h * id_rows + r, 1), :] = jnp.sum(
                        jnp.exp(x - top), axis=0, keepdims=True)

        name = jnp.concatenate([labels[g]] * (cols // 128), axis=1)
        tops = jnp.concatenate([piece_max[k] for k in range(cols // 128)], axis=1)
        sums = jnp.concatenate([piece_sum[k] for k in range(cols // 128)], axis=1)
        for r in range(RECS):
            mine = name == r
            peak = jnp.max(jnp.where(mine, tops, 0.0), axis=0, keepdims=True)
            total = jnp.sum(jnp.where(mine, sums * jnp.exp(jnp.minimum(tops - peak, 0.0)), 0.0), axis=0, keepdims=True)
            stats[g, r:r + 1, :] = log_of(peak, total)

    own_frames.wait()
    own_meta.wait()
    unfold(0)
    arrive(0)
    finish(0)
    early = chunks // 2
    for q in range(early):
        correlate(0, q)
        arrive(q + 1)
        if q + 1 < early:
            finish(q + 1)
    side_frames.wait_recv()
    side_meta.wait_recv()
    unfold(1)
    for q in range(early):
        correlate(1, q)
        if q == 1:
            arrive(early + 1)
    finish(early)
    for q in range(early, chunks):
        correlate(0, q)
        arrive(q + 2)
        if q + 1 == chunks:
            summarize(0)
            for dz in range(1, n_tm):
                start(remote(("own", dz), stats.at[0], slabs.at[z, parity], at(i, tm_plus(dz), c)))
        correlate(1, q)
        if q + 1 < chunks:
            finish(q + 1)
    summarize(1)
    for dz in range(n_tm):
        start(remote(("side", dz), stats.at[1], slabs.at[z, parity], at(side, tm_plus(dz), c)))
    slabs[z, parity] = stats[0]
    for dz in range(n_tm):
        there = slabs.at[tm_plus(-dz), 1 - parity]
        remote(("side", dz), there, there, at(side, z, c)).wait_recv()
    for dz in range(1, n_tm):
        there = slabs.at[tm_plus(-dz), parity]
        remote(("own", dz), there, there, at(i, tm_plus(-dz), c)).wait_recv()

    for h in range(2):
        peak = jnp.maximum(slabs[0, h], 0.0)
        for s in range(1, n_tm):
            peak = jnp.maximum(peak, slabs[s, h])
        total = jnp.zeros_like(peak)
        for s in range(n_tm):
            total += jnp.exp(slabs[s, h] - peak)
        rec_out[h] = peak + jnp.log(jnp.exp(-peak) + total)
        top = jnp.max(peak, axis=0, keepdims=True)
        group[h:h + 1, :] = log_of(top, jnp.sum(total * jnp.exp(peak - top), axis=0, keepdims=True))
    group[2:8, :] = jnp.zeros((6, cols), jnp.float32)

    mine = 2 * i + c
    for dj in range(n):
        for dc in range(2):
            if dj or dc:
                start(remote(("group", dj, dc), group, groups_all.at[mine],
                             at(tmpl_plus(dj), z, c if dc == 0 else 1 - c)))
    groups_all[mine] = group[...]
    for dj in range(n):
        for dc in range(2):
            if dj or dc:
                there = groups_all.at[2 * tmpl_plus(-dj) + (c if dc == 0 else 1 - c)]
                remote(("group", dj, dc), there, there, at(tmpl_plus(-dj), z, c if dc == 0 else 1 - c)).wait_recv()
    top = jnp.maximum(groups_all[0, 0:2, :], 0.0)
    for s in range(1, 2 * n):
        top = jnp.maximum(top, groups_all[s, 0:2, :])
    total = jnp.zeros_like(top)
    for s in range(2 * n):
        total += jnp.exp(groups_all[s, 0:2, :] - top)
    top_out[...] = top + jnp.log(jnp.exp(-top) + total)

    for copy in sent:
        copy.wait_send()

    @pl.when(z > 0)
    def _():
        for copy in rim_copies:
            copy.wait_send()


def on_device(n, n_tm, corpus, templates, rec_ids, valid_frames):
    rows, span, bins = templates.shape
    length = corpus.shape[1]
    halo = span
    id_rows = length // 128
    chunks = span // HALF
    depth = HALF * bins
    cols = rows * n
    meta = jnp.concatenate(
        [rec_ids.reshape(id_rows, 128), jnp.broadcast_to(valid_frames.reshape(1, 1), (8, 128))], axis=0)
    copies = 6 + chunks * n + 2 * n_tm + 2 * n
    f32, bf16, i32 = jnp.float32, jnp.bfloat16, jnp.int32
    rec_half, top_half = pl.pallas_call(
        functools.partial(kernel, n, n_tm, (span * bins) ** (-0.5)),
        out_shape=(jax.ShapeDtypeStruct((2, RECS, cols), f32), jax.ShapeDtypeStruct((2, cols), f32)),
        in_specs=[pl.BlockSpec(memory_space=pl.ANY)] * 3,
        out_specs=(pl.BlockSpec(memory_space=pltpu.VMEM), pl.BlockSpec(memory_space=pltpu.VMEM)),
        scratch_shapes=[
            pltpu.VMEM((2, length + halo, bins), bf16),
            pltpu.VMEM((length + halo + SHIFTS, bins), f32),
            pltpu.VMEM((2, length + halo, SHIFTS * bins), bf16),
            pltpu.VMEM((chunks, cols, depth), bf16),
            pltpu.VMEM((2, length, cols), f32),
            pltpu.VMEM((2, id_rows + 8, 128), i32),
            pltpu.VMEM((2, 8, 128), i32),
            pltpu.VMEM((2, length, 128), f32),
            pltpu.VMEM((2, 2 * id_rows, 128), i32),
            pltpu.VMEM((cols // 128, 2 * id_rows, 128), f32),
            pltpu.VMEM((cols // 128, 2 * id_rows, 128), f32),
            pltpu.VMEM((2, RECS, cols), f32),
            pltpu.VMEM((n_tm, 2, RECS, cols), f32),
            pltpu.VMEM((8, cols), f32),
            pltpu.VMEM((2 * n, 8, cols), f32),
            pltpu.SemaphoreType.DMA((2 + chunks,)),
            pltpu.SemaphoreType.DMA((copies,)),
            pltpu.SemaphoreType.DMA((copies,)),
        ],
        compiler_params=pltpu.CompilerParams(
            collective_id=0, has_side_effects=True, vmem_limit_bytes=48 * 1024 * 1024),
    )(corpus[0], templates.reshape(rows, span * bins), meta)
    rec = rec_half.reshape(2, RECS, n // 2, 2 * rows).transpose(1, 2, 0, 3).reshape(1, RECS, n * 2 * rows)
    top = top_half.reshape(2, n // 2, 2 * rows).transpose(1, 0, 2).reshape(n * 2 * rows)
    return rec, top


def solution(mesh):
    return jax.shard_map(
        functools.partial(on_device, mesh.shape["tmpl"], mesh.shape["tm"]),
        mesh=mesh,
        in_specs=(
            P(("tmpl", "rec"), "tm", None),
            P(("tmpl", "rec"), None, None),
            P(("tmpl", "rec"), "tm"),
            P(("tmpl", "rec"), "tm"),
        ),
        out_specs=(P(("tmpl", "rec"), None, None), P()),
        check_vma=False,
    )
```

```python
import functools

import jax
import jax.numpy as jnp
from jax import lax
from jax.experimental import pallas as pl
from jax.experimental.pallas import tpu as pltpu
from jax.sharding import PartitionSpec as P

RECS = 16
SHIFTS = 16
ROWS = 1024
PIECE = 64
LOW = -1e30
MESH = pl.DeviceIdType.MESH


def kernel(
    n, n_tm, score_scale,
    corpus, bank, meta, rec_out, top_out,
    frames, wide, unfolded, weights, scores, ids, rim_ids, bias, labels,
    piece_max, piece_sum, stats, slabs, group, groups_all,
    local_sem, send_sem, recv_sem,
):
    i, z, c = lax.axis_index("tmpl"), lax.axis_index("tm"), lax.axis_index("rec")
    parity = lax.rem(i, 2)
    side = i + 1 - 2 * parity
    rows = bank.shape[0]
    length = corpus.shape[0]
    halo = frames.shape[1] - length
    chunks = weights.shape[0]
    depth = weights.shape[2]
    cols = weights.shape[1]
    id_rows = length // 128
    half = n // 2

    def at(j, zz, cc):
        return {"tmpl": j, "tm": zz, "rec": cc}

    def tmpl_plus(by):
        return lax.rem(i + by + n, n)

    def tm_plus(by):
        return lax.rem(z + by + n_tm, n_tm)

    slots = {}

    def slot(name):
        return slots.setdefault(name, len(slots))

    def remote(name, src, dst, device):
        k = slot(name)
        return pltpu.make_async_remote_copy(
            src_ref=src, dst_ref=dst, send_sem=send_sem.at[k], recv_sem=recv_sem.at[k],
            device_id=device, device_id_type=MESH,
        )

    def block(q, j, cc):
        shard = (j // 2) * 2 + cc
        return weights.at[q, pl.ds(pl.multiple_of(shard * rows, 16), rows)]

    barrier = pltpu.get_barrier_semaphore()
    partners = [at(tmpl_plus(dj), z, c if dc == 0 else 1 - c)
                for dj in range(n) for dc in range(2) if dj or dc]
    for dz in range(1, n_tm):
        partners += [at(i, tm_plus(dz), c), at(side, tm_plus(dz), c)]
    for device in partners:
        pl.semaphore_signal(barrier, inc=1, device_id=device, device_id_type=MESH)

    own_frames = pltpu.make_async_copy(corpus, frames.at[0, pl.ds(0, length)], local_sem.at[0])
    own_meta = pltpu.make_async_copy(meta, ids.at[0], local_sem.at[1])
    own_frames.start()
    own_meta.start()
    own_bank = []
    for q in range(chunks):
        own_bank.append(pltpu.make_async_copy(
            bank.at[:, pl.ds(q * depth, depth)], block(q, i, c), local_sem.at[2 + q]))
        own_bank[-1].start()

    pl.semaphore_wait(barrier, len(partners))

    sent = []

    def start(copy):
        copy.start()
        sent.append(copy)

    rim = corpus.at[pl.ds(0, halo)]
    rim_meta = meta.at[pl.ds(0, 8)]
    before, after = tm_plus(-1), tm_plus(1)
    rim_copies = []
    for g, j in ((0, i), (1, side)):
        rim_copies.append(remote(("rim", g), rim, frames.at[g, pl.ds(length, halo)], at(j, before, c)))
        rim_copies.append(remote(("rim_ids", g), rim_meta, rim_ids.at[g], at(j, before, c)))

    @pl.when(z > 0)
    def _():
        for copy in rim_copies:
            copy.start()

    @pl.when(z == n_tm - 1)
    def _():
        for g in range(2):
            frames[g, pl.ds(length, halo), :] = jnp.zeros((halo, frames.shape[2]), jnp.bfloat16)
            rim_ids[g] = jnp.full(rim_ids.shape[1:], -1, jnp.int32)

    side_meta = remote("meta", meta, ids.at[1], at(side, z, c))
    start(side_meta)
    side_frames = remote("frames", corpus, frames.at[1, pl.ds(0, length)], at(side, z, c))
    for q in range(chunks):
        part = bank.at[:, pl.ds(q * depth, depth)]
        for d in range(1, half):
            start(remote(("bank", q, d), part, block(q, i, c), at(tmpl_plus(2 * d), z, c)))
        start(remote(("core", q), part, block(q, i, c), at(i, z, 1 - c)))
        if q == 0:
            start(side_frames)

    def arrive_bank(q):
        for d in range(1, half):
            j = tmpl_plus(-2 * d)
            remote(("bank", q, d), block(q, j, c), block(q, j, c), at(j, z, c)).wait_recv()
            start(remote(("pass", q, d), block(q, j, c), block(q, j, c), at(i, z, 1 - c)))

    def finish_bank(q):
        own_bank[q].wait()
        here = block(q, i, 1 - c)
        remote(("core", q), here, here, at(i, z, 1 - c)).wait_recv()
        for d in range(1, half):
            there = block(q, tmpl_plus(-2 * d), 1 - c)
            remote(("pass", q, d), there, there, at(i, z, 1 - c)).wait_recv()

    def unfold(g):
        @pl.when(z < n_tm - 1)
        def _():
            rim_copies[2 * g].wait_recv()
            rim_copies[2 * g + 1].wait_recv()

        total = length + halo
        wide[pl.ds(total, SHIFTS), :] = jnp.zeros((SHIFTS, wide.shape[1]), jnp.float32)

        @pl.loop(0, total // 64)
        def _(step):
            here = pl.ds(pl.multiple_of(step * 64, 64), 64)
            wide[here, :] = frames[g, here, :].astype(jnp.float32)

        @pl.loop(0, total // 64)
        def _(step):
            base = pl.multiple_of(step * 64, 64)
            for s in range(SHIFTS):
                unfolded[g, pl.ds(base, 64), s * 128:(s + 1) * 128] = (
                    wide[pl.ds(base + s, 64), :].astype(jnp.bfloat16))

        now = ids[g, 0:id_rows, :]
        rolled = pltpu.roll(now, 128 - (PIECE - 1), 1)
        rolled_rim = pltpu.roll(rim_ids[g], 128 - (PIECE - 1), 1)
        next_row = jnp.concatenate([rolled[1:], rolled_rim[0:1]], axis=0)
        lane = lax.broadcasted_iota(jnp.int32, now.shape, 1)
        row = lax.broadcasted_iota(jnp.int32, now.shape, 0)
        last = jnp.where(lane < 128 - (PIECE - 1), rolled, next_row)
        valid = ids[g, id_rows:id_rows + 1, :]
        usable = (now == last) & (row * 128 + lane < valid)
        flat = jnp.where(usable, 0.0, LOW)
        flat = jnp.concatenate([flat, jnp.zeros((128 - id_rows, 128), jnp.float32)], axis=0)
        turned = flat.T
        for r in range(id_rows):
            bias[g, r * 128:(r + 1) * 128, :] = jnp.broadcast_to(turned[:, r:r + 1], (128, 128))
        named = jnp.where(usable, now, -1)
        first = jnp.max(jnp.where(lane < PIECE, named, -1), axis=1, keepdims=True)
        second = jnp.max(jnp.where(lane >= PIECE, named, -1), axis=1, keepdims=True)
        labels[g, 0:id_rows, :] = jnp.broadcast_to(first, (id_rows, 128))
        labels[g, id_rows:2 * id_rows, :] = jnp.broadcast_to(second, (id_rows, 128))

    def correlate(g, q):
        @pl.loop(0, length // ROWS)
        def _(step):
            base = pl.multiple_of(step * ROWS, ROWS)
            part = lax.dot_general(
                unfolded[g, pl.ds(pl.multiple_of(base + q * SHIFTS, SHIFTS), ROWS), :], weights[q],
                (((1,), (1,)), ((), ())), preferred_element_type=jnp.float32)
            if q == 0:
                scores[g, pl.ds(base, ROWS), :] = part
            else:
                scores[g, pl.ds(base, ROWS), :] += part

    def log_of(peak, total):
        return jnp.where(total > 0.0, peak + jnp.log(total), LOW)

    def summarize(g):
        @pl.loop(0, id_rows, unroll=2)
        def _(r):
            for h in range(2):
                base = pl.multiple_of(r * 128 + h * PIECE, PIECE)
                mask = bias[g, pl.ds(base, PIECE), :]
                for k in range(0, cols, 128):
                    x = scores[g, pl.ds(base, PIECE), k:k + 128] * score_scale + mask
                    top = jnp.maximum(jnp.max(x, axis=0, keepdims=True), 0.0)
                    piece_max[k // 128, pl.ds(h * id_rows + r, 1), :] = top
                    piece_sum[k // 128, pl.ds(h * id_rows + r, 1), :] = jnp.sum(
                        jnp.exp(x - top), axis=0, keepdims=True)

        name = jnp.concatenate([labels[g]] * (cols // 128), axis=1)
        tops = jnp.concatenate([piece_max[k] for k in range(cols // 128)], axis=1)
        sums = jnp.concatenate([piece_sum[k] for k in range(cols // 128)], axis=1)
        for r in range(RECS):
            mine = name == r
            peak = jnp.max(jnp.where(mine, tops, 0.0), axis=0, keepdims=True)
            total = jnp.sum(jnp.where(mine, sums * jnp.exp(jnp.minimum(tops - peak, 0.0)), 0.0), axis=0, keepdims=True)
            stats[g, r:r + 1, :] = log_of(peak, total)

    own_frames.wait()
    own_meta.wait()
    unfold(0)
    arrive_bank(0)
    finish_bank(0)
    for q in range(chunks - 1):
        correlate(0, q)
        arrive_bank(q + 1)
        if q == 0:
            side_frames.wait_recv()
            side_meta.wait_recv()
            unfold(1)
        correlate(1, q)
        finish_bank(q + 1)
    correlate(1, chunks - 1)
    summarize(1)
    for dz in range(n_tm):
        start(remote(("side", dz), stats.at[1], slabs.at[z, parity], at(side, tm_plus(dz), c)))
    correlate(0, chunks - 1)
    summarize(0)
    for dz in range(1, n_tm):
        start(remote(("own", dz), stats.at[0], slabs.at[z, parity], at(i, tm_plus(dz), c)))
    slabs[z, parity] = stats[0]
    for dz in range(n_tm):
        there = slabs.at[tm_plus(-dz), 1 - parity]
        remote(("side", dz), there, there, at(side, z, c)).wait_recv()
    for dz in range(1, n_tm):
        there = slabs.at[tm_plus(-dz), parity]
        remote(("own", dz), there, there, at(i, tm_plus(-dz), c)).wait_recv()

    for h in range(2):
        peak = jnp.maximum(slabs[0, h], 0.0)
        for s in range(1, n_tm):
            peak = jnp.maximum(peak, slabs[s, h])
        total = jnp.zeros_like(peak)
        for s in range(n_tm):
            total += jnp.exp(slabs[s, h] - peak)
        rec_out[h] = peak + jnp.log(jnp.exp(-peak) + total)
        top = jnp.max(peak, axis=0, keepdims=True)
        group[h:h + 1, :] = log_of(top, jnp.sum(total * jnp.exp(peak - top), axis=0, keepdims=True))
    group[2:8, :] = jnp.zeros((6, cols), jnp.float32)

    mine = 2 * i + c
    for dj in range(n):
        for dc in range(2):
            if dj or dc:
                start(remote(("group", dj, dc), group, groups_all.at[mine],
                             at(tmpl_plus(dj), z, c if dc == 0 else 1 - c)))
    groups_all[mine] = group[...]
    for dj in range(n):
        for dc in range(2):
            if dj or dc:
                there = groups_all.at[2 * tmpl_plus(-dj) + (c if dc == 0 else 1 - c)]
                remote(("group", dj, dc), there, there, at(tmpl_plus(-dj), z, c if dc == 0 else 1 - c)).wait_recv()
    top = jnp.maximum(groups_all[0, 0:2, :], 0.0)
    for s in range(1, 2 * n):
        top = jnp.maximum(top, groups_all[s, 0:2, :])
    total = jnp.zeros_like(top)
    for s in range(2 * n):
        total += jnp.exp(groups_all[s, 0:2, :] - top)
    top_out[...] = top + jnp.log(jnp.exp(-top) + total)

    for copy in sent:
        copy.wait_send()

    @pl.when(z > 0)
    def _():
        for copy in rim_copies:
            copy.wait_send()


def on_device(n, n_tm, corpus, templates, rec_ids, valid_frames):
    rows, span, bins = templates.shape
    length = corpus.shape[1]
    halo = span
    id_rows = length // 128
    chunks = span // SHIFTS
    depth = SHIFTS * bins
    cols = rows * n
    meta = jnp.concatenate(
        [rec_ids.reshape(id_rows, 128), jnp.broadcast_to(valid_frames.reshape(1, 1), (8, 128))], axis=0)
    copies = 5 + chunks * n + 2 * n_tm + 2 * n
    f32, bf16, i32 = jnp.float32, jnp.bfloat16, jnp.int32
    rec_half, top_half = pl.pallas_call(
        functools.partial(kernel, n, n_tm, (span * bins) ** (-0.5)),
        out_shape=(jax.ShapeDtypeStruct((2, RECS, cols), f32), jax.ShapeDtypeStruct((2, cols), f32)),
        in_specs=[pl.BlockSpec(memory_space=pl.ANY)] * 3,
        out_specs=(pl.BlockSpec(memory_space=pltpu.VMEM), pl.BlockSpec(memory_space=pltpu.VMEM)),
        scratch_shapes=[
            pltpu.VMEM((2, length + halo, bins), bf16),
            pltpu.VMEM((length + halo + SHIFTS, bins), f32),
            pltpu.VMEM((2, length + halo, depth), bf16),
            pltpu.VMEM((chunks, cols, depth), bf16),
            pltpu.VMEM((2, length, cols), f32),
            pltpu.VMEM((2, id_rows + 8, 128), i32),
            pltpu.VMEM((2, 8, 128), i32),
            pltpu.VMEM((2, length, 128), f32),
            pltpu.VMEM((2, 2 * id_rows, 128), i32),
            pltpu.VMEM((cols // 128, 2 * id_rows, 128), f32),
            pltpu.VMEM((cols // 128, 2 * id_rows, 128), f32),
            pltpu.VMEM((2, RECS, cols), f32),
            pltpu.VMEM((n_tm, 2, RECS, cols), f32),
            pltpu.VMEM((8, cols), f32),
            pltpu.VMEM((2 * n, 8, cols), f32),
            pltpu.SemaphoreType.DMA((2 + chunks,)),
            pltpu.SemaphoreType.DMA((copies,)),
            pltpu.SemaphoreType.DMA((copies,)),
        ],
        compiler_params=pltpu.CompilerParams(
            collective_id=0, has_side_effects=True, vmem_limit_bytes=48 * 1024 * 1024),
    )(corpus[0], templates.reshape(rows, span * bins), meta)
    rec = rec_half.reshape(2, RECS, n // 2, 2 * rows).transpose(1, 2, 0, 3).reshape(1, RECS, n * 2 * rows)
    top = top_half.reshape(2, n // 2, 2 * rows).transpose(1, 0, 2).reshape(n * 2 * rows)
    return rec, top


def solution(mesh):
    return jax.shard_map(
        functools.partial(on_device, mesh.shape["tmpl"], mesh.shape["tm"]),
        mesh=mesh,
        in_specs=(
            P(("tmpl", "rec"), "tm", None),
            P(("tmpl", "rec"), None, None),
            P(("tmpl", "rec"), "tm"),
            P(("tmpl", "rec"), "tm"),
        ),
        out_specs=(P(("tmpl", "rec"), None, None), P()),
        check_vma=False,
    )
```

```python
import functools

import jax
import jax.numpy as jnp
from jax import lax
from jax.experimental import pallas as pl
from jax.experimental.pallas import tpu as pltpu
from jax.sharding import PartitionSpec as P

RECS = 16
SHIFTS = 16
ROWS = 1024
PIECE = 64
LOW = -1e30
MESH = pl.DeviceIdType.MESH


def kernel(
    n, n_tm, score_scale,
    corpus, bank, meta, rec_out, top_out,
    frames, wide, unfolded, weights, scores, ids, rim_ids, bias, labels,
    piece_max, piece_sum, stats, slabs, group, groups_all,
    local_sem, send_sem, recv_sem,
):
    i, z, c = lax.axis_index("tmpl"), lax.axis_index("tm"), lax.axis_index("rec")
    parity = lax.rem(i, 2)
    side = i + 1 - 2 * parity
    rows = bank.shape[0]
    length = corpus.shape[0]
    halo = frames.shape[1] - length
    chunks = weights.shape[0]
    depth = weights.shape[2]
    cols = weights.shape[1]
    id_rows = length // 128
    half = n // 2

    def at(j, zz, cc):
        return {"tmpl": j, "tm": zz, "rec": cc}

    def tmpl_plus(by):
        return lax.rem(i + by + n, n)

    def tm_plus(by):
        return lax.rem(z + by + n_tm, n_tm)

    slots = {}

    def slot(name):
        return slots.setdefault(name, len(slots))

    def remote(name, src, dst, device):
        k = slot(name)
        return pltpu.make_async_remote_copy(
            src_ref=src, dst_ref=dst, send_sem=send_sem.at[k], recv_sem=recv_sem.at[k],
            device_id=device, device_id_type=MESH,
        )

    def block(q, j, cc):
        shard = (j // 2) * 2 + cc
        return weights.at[q, pl.ds(pl.multiple_of(shard * rows, 16), rows)]

    barrier = pltpu.get_barrier_semaphore()
    partners = [at(tmpl_plus(dj), z, c if dc == 0 else 1 - c)
                for dj in range(n) for dc in range(2) if dj or dc]
    for dz in range(1, n_tm):
        partners += [at(i, tm_plus(dz), c), at(side, tm_plus(dz), c)]
    for device in partners:
        pl.semaphore_signal(barrier, inc=1, device_id=device, device_id_type=MESH)

    own_frames = pltpu.make_async_copy(corpus, frames.at[0, pl.ds(0, length)], local_sem.at[0])
    own_meta = pltpu.make_async_copy(meta, ids.at[0], local_sem.at[1])
    own_frames.start()
    own_meta.start()
    own_bank = []
    for q in range(chunks):
        own_bank.append(pltpu.make_async_copy(
            bank.at[:, pl.ds(q * depth, depth)], block(q, i, c), local_sem.at[2 + q]))
        own_bank[-1].start()

    pl.semaphore_wait(barrier, len(partners))

    sent = []

    def start(copy):
        copy.start()
        sent.append(copy)

    rim = corpus.at[pl.ds(0, halo)]
    rim_meta = meta.at[pl.ds(0, 8)]
    before, after = tm_plus(-1), tm_plus(1)
    rim_copies = []
    for g, j in ((0, i), (1, side)):
        rim_copies.append(remote(("rim", g), rim, frames.at[g, pl.ds(length, halo)], at(j, before, c)))
        rim_copies.append(remote(("rim_ids", g), rim_meta, rim_ids.at[g], at(j, before, c)))

    @pl.when(z > 0)
    def _():
        for copy in rim_copies:
            copy.start()

    @pl.when(z == n_tm - 1)
    def _():
        for g in range(2):
            frames[g, pl.ds(length, halo), :] = jnp.zeros((halo, frames.shape[2]), jnp.bfloat16)
            rim_ids[g] = jnp.full(rim_ids.shape[1:], -1, jnp.int32)

    side_meta = remote("meta", meta, ids.at[1], at(side, z, c))
    start(side_meta)
    side_frames = remote("frames", corpus, frames.at[1, pl.ds(0, length)], at(side, z, c))
    for q in range(chunks):
        part = bank.at[:, pl.ds(q * depth, depth)]
        for d in range(1, half):
            start(remote(("bank", q, d), part, block(q, i, c), at(tmpl_plus(2 * d), z, c)))
        start(remote(("core", q), part, block(q, i, c), at(i, z, 1 - c)))
        if q == 0:
            start(side_frames)

    def arrive_bank(q):
        for d in range(1, half):
            j = tmpl_plus(-2 * d)
            remote(("bank", q, d), block(q, j, c), block(q, j, c), at(j, z, c)).wait_recv()
            start(remote(("pass", q, d), block(q, j, c), block(q, j, c), at(i, z, 1 - c)))

    def finish_bank(q):
        own_bank[q].wait()
        here = block(q, i, 1 - c)
        remote(("core", q), here, here, at(i, z, 1 - c)).wait_recv()
        for d in range(1, half):
            there = block(q, tmpl_plus(-2 * d), 1 - c)
            remote(("pass", q, d), there, there, at(i, z, 1 - c)).wait_recv()

    def unfold(g):
        @pl.when(z < n_tm - 1)
        def _():
            rim_copies[2 * g].wait_recv()
            rim_copies[2 * g + 1].wait_recv()

        total = length + halo
        wide[pl.ds(total, SHIFTS), :] = jnp.zeros((SHIFTS, wide.shape[1]), jnp.float32)

        @pl.loop(0, total // 64)
        def _(step):
            here = pl.ds(pl.multiple_of(step * 64, 64), 64)
            wide[here, :] = frames[g, here, :].astype(jnp.float32)

        @pl.loop(0, total // 64)
        def _(step):
            base = pl.multiple_of(step * 64, 64)
            for s in range(SHIFTS):
                unfolded[g, pl.ds(base, 64), s * 128:(s + 1) * 128] = (
                    wide[pl.ds(base + s, 64), :].astype(jnp.bfloat16))

        now = ids[g, 0:id_rows, :]
        rolled = pltpu.roll(now, 128 - (PIECE - 1), 1)
        rolled_rim = pltpu.roll(rim_ids[g], 128 - (PIECE - 1), 1)
        next_row = jnp.concatenate([rolled[1:], rolled_rim[0:1]], axis=0)
        lane = lax.broadcasted_iota(jnp.int32, now.shape, 1)
        row = lax.broadcasted_iota(jnp.int32, now.shape, 0)
        last = jnp.where(lane < 128 - (PIECE - 1), rolled, next_row)
        valid = ids[g, id_rows:id_rows + 1, :]
        usable = (now == last) & (row * 128 + lane < valid)
        flat = jnp.where(usable, 0.0, LOW)
        flat = jnp.concatenate([flat, jnp.zeros((128 - id_rows, 128), jnp.float32)], axis=0)
        turned = flat.T
        for r in range(id_rows):
            bias[g, r * 128:(r + 1) * 128, :] = jnp.broadcast_to(turned[:, r:r + 1], (128, 128))
        named = jnp.where(usable, now, -1)
        first = jnp.max(jnp.where(lane < PIECE, named, -1), axis=1, keepdims=True)
        second = jnp.max(jnp.where(lane >= PIECE, named, -1), axis=1, keepdims=True)
        labels[g, 0:id_rows, :] = jnp.broadcast_to(first, (id_rows, 128))
        labels[g, id_rows:2 * id_rows, :] = jnp.broadcast_to(second, (id_rows, 128))

    def correlate(g, q):
        @pl.loop(0, length // ROWS)
        def _(step):
            base = pl.multiple_of(step * ROWS, ROWS)
            part = lax.dot_general(
                unfolded[g, pl.ds(pl.multiple_of(base + q * SHIFTS, SHIFTS), ROWS), :], weights[q],
                (((1,), (1,)), ((), ())), preferred_element_type=jnp.float32)
            if q == 0:
                scores[g, pl.ds(base, ROWS), :] = part
            else:
                scores[g, pl.ds(base, ROWS), :] += part

    def log_of(peak, total):
        return jnp.where(total > 0.0, peak + jnp.log(total), LOW)

    def summarize(g):
        @pl.loop(0, id_rows, unroll=4)
        def _(r):
            for h in range(2):
                base = pl.multiple_of(r * 128 + h * PIECE, PIECE)
                mask = bias[g, pl.ds(base, PIECE), :]
                for k in range(0, cols, 128):
                    x = scores[g, pl.ds(base, PIECE), k:k + 128] * score_scale + mask
                    top = jnp.maximum(jnp.max(x, axis=0, keepdims=True), 0.0)
                    piece_max[k // 128, pl.ds(h * id_rows + r, 1), :] = top
                    piece_sum[k // 128, pl.ds(h * id_rows + r, 1), :] = jnp.sum(
                        jnp.exp(x - top), axis=0, keepdims=True)

        name = jnp.concatenate([labels[g]] * (cols // 128), axis=1)
        tops = jnp.concatenate([piece_max[k] for k in range(cols // 128)], axis=1)
        sums = jnp.concatenate([piece_sum[k] for k in range(cols // 128)], axis=1)
        for r in range(RECS):
            mine = name == r
            peak = jnp.max(jnp.where(mine, tops, 0.0), axis=0, keepdims=True)
            total = jnp.sum(jnp.where(mine, sums * jnp.exp(jnp.minimum(tops - peak, 0.0)), 0.0), axis=0, keepdims=True)
            stats[g, r:r + 1, :] = log_of(peak, total)

    own_frames.wait()
    own_meta.wait()
    unfold(0)
    arrive_bank(0)
    finish_bank(0)
    for q in range(chunks - 1):
        correlate(0, q)
        arrive_bank(q + 1)
        if q == 0:
            side_frames.wait_recv()
            side_meta.wait_recv()
            unfold(1)
        correlate(1, q)
        finish_bank(q + 1)
    correlate(1, chunks - 1)
    summarize(1)
    for dz in range(n_tm):
        start(remote(("side", dz), stats.at[1], slabs.at[z, parity], at(side, tm_plus(dz), c)))
    correlate(0, chunks - 1)
    summarize(0)
    for dz in range(1, n_tm):
        start(remote(("own", dz), stats.at[0], slabs.at[z, parity], at(i, tm_plus(dz), c)))
    slabs[z, parity] = stats[0]
    for dz in range(n_tm):
        there = slabs.at[tm_plus(-dz), 1 - parity]
        remote(("side", dz), there, there, at(side, z, c)).wait_recv()
    for dz in range(1, n_tm):
        there = slabs.at[tm_plus(-dz), parity]
        remote(("own", dz), there, there, at(i, tm_plus(-dz), c)).wait_recv()

    for h in range(2):
        peak = jnp.maximum(slabs[0, h], 0.0)
        for s in range(1, n_tm):
            peak = jnp.maximum(peak, slabs[s, h])
        total = jnp.zeros_like(peak)
        for s in range(n_tm):
            total += jnp.exp(slabs[s, h] - peak)
        rec_out[h] = peak + jnp.log(jnp.exp(-peak) + total)
        top = jnp.max(peak, axis=0, keepdims=True)
        group[h:h + 1, :] = log_of(top, jnp.sum(total * jnp.exp(peak - top), axis=0, keepdims=True))
    group[2:8, :] = jnp.zeros((6, cols), jnp.float32)

    mine = 2 * i + c
    for dj in range(n):
        for dc in range(2):
            if dj or dc:
                start(remote(("group", dj, dc), group, groups_all.at[mine],
                             at(tmpl_plus(dj), z, c if dc == 0 else 1 - c)))
    groups_all[mine] = group[...]
    for dj in range(n):
        for dc in range(2):
            if dj or dc:
                there = groups_all.at[2 * tmpl_plus(-dj) + (c if dc == 0 else 1 - c)]
                remote(("group", dj, dc), there, there, at(tmpl_plus(-dj), z, c if dc == 0 else 1 - c)).wait_recv()
    top = jnp.maximum(groups_all[0, 0:2, :], 0.0)
    for s in range(1, 2 * n):
        top = jnp.maximum(top, groups_all[s, 0:2, :])
    total = jnp.zeros_like(top)
    for s in range(2 * n):
        total += jnp.exp(groups_all[s, 0:2, :] - top)
    top_out[...] = top + jnp.log(jnp.exp(-top) + total)

    for copy in sent:
        copy.wait_send()

    @pl.when(z > 0)
    def _():
        for copy in rim_copies:
            copy.wait_send()


def on_device(n, n_tm, corpus, templates, rec_ids, valid_frames):
    rows, span, bins = templates.shape
    length = corpus.shape[1]
    halo = span
    id_rows = length // 128
    chunks = span // SHIFTS
    depth = SHIFTS * bins
    cols = rows * n
    meta = jnp.concatenate(
        [rec_ids.reshape(id_rows, 128), jnp.broadcast_to(valid_frames.reshape(1, 1), (8, 128))], axis=0)
    copies = 5 + chunks * n + 2 * n_tm + 2 * n
    f32, bf16, i32 = jnp.float32, jnp.bfloat16, jnp.int32
    rec_half, top_half = pl.pallas_call(
        functools.partial(kernel, n, n_tm, (span * bins) ** (-0.5)),
        out_shape=(jax.ShapeDtypeStruct((2, RECS, cols), f32), jax.ShapeDtypeStruct((2, cols), f32)),
        in_specs=[pl.BlockSpec(memory_space=pl.ANY)] * 3,
        out_specs=(pl.BlockSpec(memory_space=pltpu.VMEM), pl.BlockSpec(memory_space=pltpu.VMEM)),
        scratch_shapes=[
            pltpu.VMEM((2, length + halo, bins), bf16),
            pltpu.VMEM((length + halo + SHIFTS, bins), f32),
            pltpu.VMEM((2, length + halo, depth), bf16),
            pltpu.VMEM((chunks, cols, depth), bf16),
            pltpu.VMEM((2, length, cols), f32),
            pltpu.VMEM((2, id_rows + 8, 128), i32),
            pltpu.VMEM((2, 8, 128), i32),
            pltpu.VMEM((2, length, 128), f32),
            pltpu.VMEM((2, 2 * id_rows, 128), i32),
            pltpu.VMEM((cols // 128, 2 * id_rows, 128), f32),
            pltpu.VMEM((cols // 128, 2 * id_rows, 128), f32),
            pltpu.VMEM((2, RECS, cols), f32),
            pltpu.VMEM((n_tm, 2, RECS, cols), f32),
            pltpu.VMEM((8, cols), f32),
            pltpu.VMEM((2 * n, 8, cols), f32),
            pltpu.SemaphoreType.DMA((2 + chunks,)),
            pltpu.SemaphoreType.DMA((copies,)),
            pltpu.SemaphoreType.DMA((copies,)),
        ],
        compiler_params=pltpu.CompilerParams(
            collective_id=0, has_side_effects=True, vmem_limit_bytes=48 * 1024 * 1024),
    )(corpus[0], templates.reshape(rows, span * bins), meta)
    rec = rec_half.reshape(2, RECS, n // 2, 2 * rows).transpose(1, 2, 0, 3).reshape(1, RECS, n * 2 * rows)
    top = top_half.reshape(2, n // 2, 2 * rows).transpose(1, 0, 2).reshape(n * 2 * rows)
    return rec, top


def solution(mesh):
    return jax.shard_map(
        functools.partial(on_device, mesh.shape["tmpl"], mesh.shape["tm"]),
        mesh=mesh,
        in_specs=(
            P(("tmpl", "rec"), "tm", None),
            P(("tmpl", "rec"), None, None),
            P(("tmpl", "rec"), "tm"),
            P(("tmpl", "rec"), "tm"),
        ),
        out_specs=(P(("tmpl", "rec"), None, None), P()),
        check_vma=False,
    )
```
